256 devices in a mesh: wide: 64 (over y_lo, x, z), feat: 4 (over y_hi, core).
Axes of the slice: x: 4, y: 4 (y_hi: 2, y_lo: 2; y = y_hi * 2 + y_lo), z: 8, core: 2. Of those that a mesh axis runs over, the one named last changes fastest.
Arguments:
- features: bfloat16 [131072, 8192], P('wide', 'feat'), may hold values from -6 to 6
- queries: bfloat16 [128, 8192], replicated, may hold values from -0.0625 to 0.0625
- inverse_factor: bfloat16 [4, 2048, 8192], P('feat', 'wide'), may hold values from -0.3 to 1
Outputs:
- scores: float32 [131072, 128], P(('wide', 'feat'))
The draws below stay inside these ranges and needn't reach their ends.
All inputs are finite; a program needn't handle non-finite values.
Results may differ from the reference program's by a relative error of at most 0.015.
Values may be sent and summed in bfloat16 or wider, within the bound.
No kernel may reach another device: no remote copies, remote signals or barrier semaphores. Data moves between devices by JAX's collectives and lax.ppermute only.
A program may use at most 64 MiB of HBM per device.

```python
import math
import jax
import jax.numpy as jnp

K = 8192
M = 128
ROWS = 131072
FEAT_COLS = 2048


def draw_inverse_factor(key, part):
    key = jax.random.fold_in(key, 7)
    noise_key, diag_key = jax.random.split(key)
    noise = jax.random.normal(noise_key, (K, K), jnp.float32) * (0.6 / math.sqrt(K))
    diagonal = jax.random.uniform(diag_key, (K,), jnp.float32, 0.3, 0.8)
    index = jnp.arange(K)
    full = noise + jnp.where(index[:, None] == index[None, :], diagonal[:, None], 0.0)
    full = jnp.clip(full, -0.3, 1.0)
    return full.reshape(K // FEAT_COLS, FEAT_COLS, K).astype(jnp.bfloat16)


def shard_levels(own_key, shape, cuts, least, high):
    loudness = 1.0
    for dim, blocks in cuts:
        draws = jax.random.uniform(jax.random.fold_in(jax.random.fold_in(own_key, 6), dim), (blocks,), jnp.float32, least / len(cuts), high / len(cuts))
        loudness = loudness * jnp.repeat(jnp.exp(draws), shape[dim] // blocks).reshape((-1,) + (1,) * (len(shape) - 1 - dim))
    return loudness


def gaussian(key, extent, deviation, limit, shards=(), held_as=jnp.bfloat16):
    loudness = shard_levels(key, extent, shards, -0.22, 0.18) if shards else 1.0
    result = jax.random.normal(key, extent, jnp.float32) * deviation * loudness
    return jnp.minimum(jnp.maximum(result, -limit), limit).astype(held_as)


def setup_inputs(seed: int = 0) -> dict:
    streams_of = jax.random.split(jax.random.key(seed), 4)
    return {
        "features": gaussian(streams_of[0], (ROWS, K), 1.0, 6.0, ((0, 64), (1, 4))),
        "queries": gaussian(streams_of[1], (M, K), K ** -0.5, 0.0625),
        "inverse_factor": draw_inverse_factor(jax.random.fold_in(streams_of[3], 71), 0),
    }


def reference(features, queries, inverse_factor):
    factor = inverse_factor.reshape(K, K)
    precond = jnp.dot(factor, queries.T, preferred_element_type=jnp.float32)
    precond_half = precond.astype(jnp.bfloat16)
    row_weights = jnp.dot(features, precond_half, preferred_element_type=jnp.float32).astype(jnp.bfloat16)
    gram_image = jnp.dot(features.T, row_weights, preferred_element_type=jnp.float32)
    residual = (gram_image / ROWS + 0.1 * precond).astype(jnp.bfloat16)
    corrected = (2.0 * precond - jnp.dot(factor, residual, preferred_element_type=jnp.float32)).astype(jnp.bfloat16)
    return jnp.dot(features, corrected, preferred_element_type=jnp.float32)
```

```python
import jax
import jax.numpy as jnp
from jax import lax
from jax.sharding import PartitionSpec as P

CORE_SWAP = [(0, 1), (1, 0), (2, 3), (3, 2)]
CHIP_SWAP = [(0, 2), (2, 0), (1, 3), (3, 1)]


def swap_core(block):
    return lax.ppermute(block, "feat", CORE_SWAP)


def swap_chip(block):
    return lax.ppermute(block, "feat", CHIP_SWAP)


def gather_wide(block):
    width = lax.axis_size("wide")
    copies = jnp.tile(block, (width, 1))
    return lax.all_to_all(copies, "wide", 0, 0, tiled=True)


def half(block, which, axis=0):
    size = block.shape[axis] // 2
    return lax.dynamic_slice_in_dim(block, which * size, size, axis)


def on_device(features, queries, inverse_factor):
    f32, bf16 = jnp.float32, jnp.bfloat16
    factor = inverse_factor[0]
    width = lax.axis_size("wide")
    row_count, cols = features.shape
    depth = factor.shape[0]
    total_rows = row_count * width
    place = lax.axis_index("feat")
    chip, core = place // 2, place % 2

    by_core = factor.reshape(depth, 2, 2, cols).transpose(2, 1, 0, 3)
    keep = lax.dynamic_index_in_dim(by_core, core, 0, keepdims=False)
    give = lax.dynamic_index_in_dim(by_core, 1 - core, 0, keepdims=False)
    got = swap_core(give)
    both = jnp.where(core == 0, jnp.stack([keep, got], 1), jnp.stack([got, keep], 1))
    keep = lax.dynamic_index_in_dim(both, chip, 0, keepdims=False)
    give = lax.dynamic_index_in_dim(both, 1 - chip, 0, keepdims=False)
    got = swap_chip(give)
    own_cols = jnp.where(chip == 0, jnp.stack([keep, got]), jnp.stack([got, keep]))
    own_cols = own_cols.reshape(4 * depth, cols)

    query_block = jnp.einsum("kc,mc->km", factor, queries, preferred_element_type=f32)
    query_cols = gather_wide(query_block.astype(bf16))

    partial = jnp.dot(features, query_cols, preferred_element_type=f32).astype(bf16)
    got = swap_core(half(partial, 1 - core))
    chip_sum = (half(partial, core).astype(f32) + got.astype(f32)).astype(bf16)
    got = swap_chip(chip_sum)
    mine = (chip_sum.astype(f32) + got.astype(f32)).astype(bf16)
    other = swap_core(mine)
    row_weights = jnp.concatenate(
        [jnp.where(core == 0, mine, other), jnp.where(core == 0, other, mine)], 0
    )

    gram_part = jnp.einsum("nk,nm->km", features, row_weights, preferred_element_type=f32)
    gram_parts = lax.all_to_all(gram_part.astype(bf16), "wide", 0, 0, tiled=True)
    gram_block = jnp.sum(gram_parts.reshape(width, depth, -1).astype(f32), axis=0)
    residual_block = (gram_block / total_rows + 0.1 * query_block).astype(bf16)
    residual_cols = gather_wide(residual_block)

    product = jnp.dot(own_cols, residual_cols, preferred_element_type=f32)
    product = product.reshape(2, 2, depth, -1)
    give = lax.dynamic_index_in_dim(product, 1 - core, 1, keepdims=False)
    keep = lax.dynamic_index_in_dim(product, core, 1, keepdims=False)
    product = keep + swap_core(give)
    give = lax.dynamic_index_in_dim(product, 1 - chip, 0, keepdims=False)
    keep = lax.dynamic_index_in_dim(product, chip, 0, keepdims=False)
    product = keep + swap_chip(give)
    corrected_block = (2.0 * query_block - product).astype(bf16)
    corrected_cols = gather_wide(corrected_block)

    partial = jnp.dot(features, corrected_cols, preferred_element_type=f32).astype(bf16)
    quarters = partial.reshape(2, 2, row_count // 4, -1)
    give = lax.dynamic_index_in_dim(quarters, 1 - core, 1, keepdims=False)
    keep = lax.dynamic_index_in_dim(quarters, core, 1, keepdims=False)
    chip_sum = keep.astype(f32) + swap_core(give).astype(f32)
    give = lax.dynamic_index_in_dim(chip_sum, 1 - chip, 0, keepdims=False).astype(bf16)
    keep = lax.dynamic_index_in_dim(chip_sum, chip, 0, keepdims=False)
    return keep + swap_chip(give).astype(f32)


def solution(mesh):
    in_specs = (P("wide", "feat"), P(), P("feat", "wide", None))
    out_specs = P(("wide", "feat"), None)
    return jax.shard_map(
        on_device, mesh=mesh, in_specs=in_specs, out_specs=out_specs, check_vma=False
    )
```

```python
import functools
import jax
import jax.numpy as jnp
from jax import lax
from jax.experimental import pallas as pl
from jax.experimental.pallas import tpu as pltpu
from jax.sharding import PartitionSpec as P

CORE_SWAP = [(0, 1), (1, 0), (2, 3), (3, 2)]
CHIP_SWAP = [(0, 2), (2, 0), (1, 3), (3, 1)]
F32, BF16 = jnp.float32, jnp.bfloat16
IN_VMEM = pl.BlockSpec(memory_space=pltpu.VMEM)


def swap_core(block):
    return lax.ppermute(block, "feat", CORE_SWAP)


def swap_chip(block):
    return lax.ppermute(block, "feat", CHIP_SWAP)


def exchange_wide(blocks):
    return lax.all_to_all(blocks, "wide", 0, 0, tiled=True)


def local_call(body, operands, shapes, name):
    return pl.pallas_call(
        body,
        in_specs=[IN_VMEM] * len(operands),
        out_specs=[IN_VMEM] * len(shapes),
        out_shape=[jax.ShapeDtypeStruct(shape, dtype) for shape, dtype in shapes],
        compiler_params=pltpu.CompilerParams(vmem_limit_bytes=32 << 20),
        name=name,
    )(*operands)


def span(start, size):
    return pl.ds(pl.multiple_of(start, size), size)


def precond_body(steps, factor_ref, queries_ref, block_ref, total_ref):
    step = pl.program_id(0)

    @pl.when(step == 0)
    def _():
        total_ref[...] = jnp.zeros_like(total_ref)

    total_ref[...] += lax.dot_general(
        factor_ref[...], queries_ref[...], (((1,), (1,)), ((), ())), preferred_element_type=F32
    )

    @pl.when(step == steps - 1)
    def _():
        block_ref[...] = total_ref[...]


def precond(factor, queries):
    depth, width = factor.shape
    count = queries.shape[0]
    steps = 2
    piece = width // steps
    return pl.pallas_call(
        functools.partial(precond_body, steps),
        grid=(steps,),
        in_specs=[
            pl.BlockSpec((depth, piece), lambda i: (0, i)),
            pl.BlockSpec((count, piece), lambda i: (0, i)),
        ],
        out_specs=pl.BlockSpec((depth, count), lambda i: (0, 0)),
        out_shape=jax.ShapeDtypeStruct((depth, count), F32),
        scratch_shapes=[pltpu.VMEM((depth, count), F32)],
        name="precond",
    )(factor, queries)


def row_body(features_ref, cols_ref, give_ref, keep_ref):
    core = lax.axis_index("feat") % 2
    size = give_ref.shape[0]
    cols = cols_ref[...]
    for part, out_ref in ((1 - core, give_ref), (core, keep_ref)):
        rows = features_ref[span(part * size, size), :]
        out_ref[...] = jnp.dot(rows, cols, preferred_element_type=F32).astype(out_ref.dtype)


def gram_body(features_ref, mine_ref, other_ref, out_ref):
    core = lax.axis_index("feat") % 2
    size = mine_ref.shape[0]
    piece = 512
    mine, other = mine_ref[...].T, other_ref[...].T
    for i in range(out_ref.shape[0] // piece):
        cols = slice(i * piece, (i + 1) * piece)
        total = jnp.dot(
            mine, features_ref[span(core * size, size), cols], preferred_element_type=F32
        ) + jnp.dot(
            other, features_ref[span((1 - core) * size, size), cols], preferred_element_type=F32
        )
        out_ref[cols, :] = total.T.astype(out_ref.dtype)


def residual_body(total_rows, block_ref, parts_ref, out_ref):
    gram = jnp.sum(parts_ref[...].astype(F32), axis=0)
    residual = (gram / total_rows + 0.1 * block_ref[...]).astype(out_ref.dtype)
    out_ref[...] = jnp.broadcast_to(residual[None], out_ref.shape)


def product_body(factor_ref, cols_ref, give_ref, keep_ref):
    size = give_ref.shape[0]
    product = jnp.dot(factor_ref[...], cols_ref[...], preferred_element_type=F32)
    give_ref[...] = product[:size]
    keep_ref[...] = product[size:]


def score_body(features_ref, cols_ref, give_ref, keep_ref):
    place = lax.axis_index("feat")
    chip, core = place // 2, place % 2
    size = give_ref.shape[0] // 2
    cols = cols_ref[...]
    for whose, out_ref in ((1 - core, give_ref), (core, keep_ref)):
        for i, where in enumerate((1 - chip, chip)):
            rows = features_ref[span((where * 2 + whose) * size, size), :]
            product = jnp.dot(rows, cols, preferred_element_type=F32)
            out_ref[i * size : (i + 1) * size, :] = product.astype(out_ref.dtype)


def own_columns(factor, cols):
    place = lax.axis_index("feat")
    chip, core = place // 2, place % 2
    depth = factor.shape[0]
    by_core = factor.reshape(depth, 2, 2, cols)
    give = lax.dynamic_index_in_dim(by_core, 1 - core, 2, keepdims=False)
    keep = lax.dynamic_index_in_dim(by_core, core, 2, keepdims=False)
    both = jnp.stack([swap_core(give), keep])
    give = lax.dynamic_index_in_dim(both, 1 - chip, 2, keepdims=False)
    keep = lax.dynamic_index_in_dim(both, chip, 2, keepdims=False)
    whole = jnp.stack([swap_chip(give), keep], 1)
    return whole.reshape(4 * depth, cols)


def on_device(features, queries, inverse_factor):
    factor = inverse_factor[0]
    width = lax.axis_size("wide")
    row_count, cols = features.shape
    depth = factor.shape[0]
    count = queries.shape[0]
    total_rows = row_count * width

    query_block = precond(factor, queries)
    query_cols = exchange_wide(jnp.tile(query_block.astype(BF16), (width, 1)))
    factor_cols = own_columns(factor, cols)

    half = (row_count // 2, count)
    give, keep = local_call(row_body, (features, query_cols), [(half, BF16), (half, F32)], "rows")
    chip_sum = (keep + swap_core(give).astype(F32)).astype(BF16)
    mine = (chip_sum.astype(F32) + swap_chip(chip_sum).astype(F32)).astype(BF16)
    other = swap_core(mine)

    (gram_part,) = local_call(gram_body, (features, mine, other), [((cols, count), BF16)], "gram")
    gram_parts = exchange_wide(gram_part).reshape(width, depth, count)
    (residual,) = local_call(
        functools.partial(residual_body, total_rows),
        (query_block, gram_parts),
        [((width, depth, count), BF16)],
        "residual",
    )
    residual_cols = exchange_wide(residual.reshape(cols, count))

    part = (2 * depth, count)
    give, keep = local_call(
        product_body, (factor_cols, residual_cols), [(part, F32), (part, F32)], "product"
    )
    product = keep + swap_core(give)
    product = product[depth:] + swap_chip(product[:depth])
    corrected = (2.0 * query_block - product).astype(BF16)
    corrected_cols = exchange_wide(jnp.tile(corrected, (width, 1)))

    give, keep = local_call(
        score_body, (features, corrected_cols), [(half, BF16), (half, F32)], "scores"
    )
    scores = keep + swap_core(give).astype(F32)
    quarter = row_count // 4
    return scores[quarter:] + swap_chip(scores[:quarter].astype(BF16)).astype(F32)


def solution(mesh):
    in_specs = (P("wide", "feat"), P(), P("feat", "wide", None))
    out_specs = P(("wide", "feat"), None)
    return jax.shard_map(
        on_device, mesh=mesh, in_specs=in_specs, out_specs=out_specs, check_vma=False
    )
```

```python
import functools
import jax
import jax.numpy as jnp
from jax import lax
from jax.experimental import pallas as pl
from jax.experimental.pallas import tpu as pltpu
from jax.sharding import PartitionSpec as P

CORE_SWAP = [(0, 1), (1, 0), (2, 3), (3, 2)]
CHIP_SWAP = [(0, 2), (2, 0), (1, 3), (3, 1)]
F32, BF16 = jnp.float32, jnp.bfloat16
IN_VMEM = pl.BlockSpec(memory_space=pltpu.VMEM)


def swap_core(block):
    return lax.ppermute(block, "feat", CORE_SWAP)


def swap_chip(block):
    return lax.ppermute(block, "feat", CHIP_SWAP)


def exchange_wide(blocks):
    return lax.all_to_all(blocks, "wide", 0, 0, tiled=True)


def local_call(body, operands, shapes, name, scratch=(), outside=0, limit=8):
    anywhere = pl.BlockSpec(memory_space=pl.ANY)
    return pl.pallas_call(
        body,
        in_specs=[anywhere] * outside + [IN_VMEM] * (len(operands) - outside),
        out_specs=[IN_VMEM] * len(shapes),
        out_shape=[jax.ShapeDtypeStruct(shape, dtype) for shape, dtype in shapes],
        scratch_shapes=list(scratch),
        compiler_params=pltpu.CompilerParams(vmem_limit_bytes=limit << 20),
        name=name,
    )(*operands)


def span(start, size):
    return pl.ds(pl.multiple_of(start, size), size)


def precond_body(
    factor_hbm, queries_hbm, block_ref, tiled_ref, give_ref, keep_ref, factor_ref, queries_ref, sems
):
    place = lax.axis_index("feat")
    chip, core = place // 2, place % 2
    size = give_ref.shape[2]
    steps = 4
    size_q = factor_ref.shape[1] // steps
    factor_copies, query_copies = [], []
    for i in range(steps):
        cols = slice(i * size_q, (i + 1) * size_q)
        factor_copies.append(
            pltpu.make_async_copy(factor_hbm.at[:, cols], factor_ref.at[:, cols], sems.at[0, i])
        )
        query_copies.append(
            pltpu.make_async_copy(queries_hbm.at[:, cols], queries_ref.at[:, cols], sems.at[1, i])
        )
        factor_copies[i].start()
        query_copies[i].start()
    block = jnp.zeros_like(block_ref)
    for j in range(2):
        for i in range(j * steps // 2, (j + 1) * steps // 2):
            factor_copies[i].wait()
            query_copies[i].wait()
        piece = factor_ref.shape[1] // 2
        cols = slice(j * piece, (j + 1) * piece)
        block += lax.dot_general(
            factor_ref[:, cols],
            queries_ref[:, cols],
            (((1,), (1,)), ((), ())),
            preferred_element_type=F32,
        )
    for whose, out_ref in ((1 - core, give_ref), (core, keep_ref)):
        for i, where in enumerate((1 - chip, chip)):
            out_ref[i] = factor_ref[:, span((where * 2 + whose) * size, size)]
    block_ref[...] = block
    tiled_ref[...] = jnp.broadcast_to(block.astype(tiled_ref.dtype)[None], tiled_ref.shape)


def row_body(pieces, features_hbm, cols_ref, give_ref, keep_ref, features_ref, sems):
    core = lax.axis_index("feat") % 2
    half = give_ref.shape[0]
    steps = sems.shape[0]
    size = 2 * half // steps
    first = (1 - core) * half
    cols = cols_ref[...]
    copies = []
    for i in range(steps):
        rows = span(lax.rem(first + i * size, 2 * half), size)
        copies.append(
            pltpu.make_async_copy(features_hbm.at[rows], features_ref.at[rows], sems.at[i])
        )
    ahead = 6
    for copy in copies[:ahead]:
        copy.start()
    size = 2 * half // pieces
    for i in range(pieces):
        for j in range(i * steps // pieces, (i + 1) * steps // pieces):
            copies[j].wait()
            if j + ahead < steps:
                copies[j + ahead].start()
        rows = span(lax.rem(first + i * size, 2 * half), size)
        product = jnp.dot(features_ref[rows, :], cols, preferred_element_type=F32)
        out_ref, j = (give_ref, i) if i < pieces // 2 else (keep_ref, i - pieces // 2)
        out_ref[j * size : (j + 1) * size, :] = product.astype(out_ref.dtype)


def gram_body(features_ref, mine_ref, other_ref, out_ref, rows_ref):
    core = lax.axis_index("feat") % 2
    size = mine_ref.shape[0]
    piece = 512
    rows_ref[span(core * size, size), :] = mine_ref[...]
    rows_ref[span((1 - core) * size, size), :] = other_ref[...]
    rows = rows_ref[...].T
    for i in range(out_ref.shape[0] // piece):
        cols = slice(i * piece, (i + 1) * piece)
        total = jnp.dot(rows, features_ref[:, cols], preferred_element_type=F32)
        out_ref[cols, :] = total.T.astype(out_ref.dtype)


def residual_body(total_rows, block_ref, parts_ref, out_ref):
    gram = jnp.sum(parts_ref[...].astype(F32), axis=0)
    residual = (gram / total_rows + 0.1 * block_ref[...]).astype(out_ref.dtype)
    out_ref[...] = jnp.broadcast_to(residual[None], out_ref.shape)


def product_body(factor_ref, cols_ref, give_ref, keep_ref):
    size = give_ref.shape[0]
    product = jnp.dot(factor_ref[...], cols_ref[...], preferred_element_type=F32)
    give_ref[...] = product[:size]
    keep_ref[...] = product[size:]


def score_body(own, features_ref, cols_ref, give_ref, keep_ref):
    place = lax.axis_index("feat")
    chip, core = place // 2, place % 2
    where = chip if own else 1 - chip
    size = give_ref.shape[0]
    cols = cols_ref[...]
    for whose, out_ref in ((1 - core, give_ref), (core, keep_ref)):
        rows = features_ref[span((where * 2 + whose) * size, size), :]
        out_ref[...] = jnp.dot(rows, cols, preferred_element_type=F32).astype(out_ref.dtype)


def on_device(features, queries, inverse_factor):
    factor = inverse_factor[0]
    width = lax.axis_size("wide")
    row_count, cols = features.shape
    depth = factor.shape[0]
    count = queries.shape[0]
    total_rows = row_count * width

    query_block, tiled, give, keep = local_call(
        precond_body,
        (factor, queries),
        [((depth, count), F32), ((width, depth, count), BF16)] + [((2, depth, cols), BF16)] * 2,
        "precond",
        [
            pltpu.VMEM(factor.shape, BF16),
            pltpu.VMEM(queries.shape, BF16),
            pltpu.SemaphoreType.DMA((2, 4)),
        ],
        outside=2,
        limit=53,
        )
    query_cols = exchange_wide(tiled.reshape(cols, count))
    got = swap_core(give)
    far = swap_chip(jnp.stack([got[0], keep[0]]))
    factor_cols = jnp.stack([far[0], got[1], far[1], keep[1]]).reshape(4 * depth, cols)
    query_cols, factor_cols = lax.optimization_barrier((query_cols, factor_cols))

    half = (row_count // 2, count)
    give, keep, held = local_call(
        functools.partial(row_body, 8),
        (features, query_cols),
        [(half, BF16), (half, F32), (features.shape, BF16)],
        "rows",
        [pltpu.SemaphoreType.DMA((16,))],
        outside=1,
        limit=43,
    )
    chip_sum = (keep + swap_core(give).astype(F32)).astype(BF16)
    mine = (chip_sum.astype(F32) + swap_chip(chip_sum).astype(F32)).astype(BF16)
    other = swap_core(mine)

    (gram_part,) = local_call(
        gram_body,
        (held, mine, other),
        [((cols, count), BF16)],
        "gram",
        [pltpu.VMEM((row_count, count), BF16)],
    )
    gram_parts = exchange_wide(gram_part).reshape(width, depth, count)
    (residual,) = local_call(
        functools.partial(residual_body, total_rows),
        (query_block, gram_parts),
        [((width, depth, count), BF16)],
        "residual",
    )
    residual_cols = exchange_wide(residual.reshape(cols, count))

    part = (2 * depth, count)
    give, keep = local_call(
        product_body, (factor_cols, residual_cols), [(part, F32), (part, F32)], "product"
    )
    product = keep + swap_core(give)
    product = product[depth:] + swap_chip(product[:depth])
    corrected = (2.0 * query_block - product).astype(BF16)
    corrected_cols = exchange_wide(jnp.tile(corrected, (width, 1)))

    quarter = (row_count // 4, count)
    sums = []
    for own in (False, True):
        give, keep = local_call(
            functools.partial(score_body, own),
            (held, corrected_cols),
            [(quarter, BF16), (quarter, F32)],
            "own_scores" if own else "far_scores",
        )
        sums.append(keep + swap_core(give).astype(F32))
    return sums[1] + swap_chip(sums[0].astype(BF16)).astype(F32)


def solution(mesh):
    in_specs = (P("wide", "feat"), P(), P("feat", "wide", None))
    out_specs = P(("wide", "feat"), None)
    return jax.shard_map(
        on_device, mesh=mesh, in_specs=in_specs, out_specs=out_specs, check_vma=False
    )
```

```python
import functools
import jax
import jax.numpy as jnp
from jax import lax
from jax.experimental import pallas as pl
from jax.experimental.pallas import tpu as pltpu
from jax.sharding import PartitionSpec as P

CORE_SWAP = [(0, 1), (1, 0), (2, 3), (3, 2)]
CHIP_SWAP = [(0, 2), (2, 0), (1, 3), (3, 1)]
F32, BF16 = jnp.float32, jnp.bfloat16
IN_VMEM = pl.BlockSpec(memory_space=pltpu.VMEM)


def swap_core(block):
    return lax.ppermute(block, "feat", CORE_SWAP)


def swap_chip(block):
    return lax.ppermute(block, "feat", CHIP_SWAP)


def swap_side(block):
    width = lax.axis_size("wide")
    return lax.ppermute(block, "wide", [(i, (i + width // 2) % width) for i in range(width)])


def swap_chip_and_side(block):
    width = lax.axis_size("wide")
    pairs = [
        (i * 4 + j, (i + width // 2) % width * 4 + k) for i in range(width) for j, k in CHIP_SWAP
    ]
    return lax.ppermute(block, ("wide", "feat"), pairs)


def exchange_side(blocks):
    half = lax.axis_size("wide") // 2
    sides = [list(range(half)), list(range(half, 2 * half))]
    return lax.all_to_all(blocks, "wide", 0, 0, tiled=True, axis_index_groups=sides)


def my_side():
    return lax.axis_index("wide") // (lax.axis_size("wide") // 2)


def local_call(body, operands, shapes, name, scratch=(), outside=0, limit=8):
    anywhere = pl.BlockSpec(memory_space=pl.ANY)
    return pl.pallas_call(
        body,
        in_specs=[anywhere] * outside + [IN_VMEM] * (len(operands) - outside),
        out_specs=[IN_VMEM] * len(shapes),
        out_shape=[jax.ShapeDtypeStruct(shape, dtype) for shape, dtype in shapes],
        scratch_shapes=list(scratch),
        compiler_params=pltpu.CompilerParams(vmem_limit_bytes=limit << 20),
        name=name,
    )(*operands)


def span(start, size):
    return pl.ds(pl.multiple_of(start, size), size)


def precond_body(
    factor_hbm, queries_hbm, block_ref, tiled_ref, give_ref, keep_ref, factor_ref, queries_ref, sems
):
    place = lax.axis_index("feat")
    chip, core, side = place // 2, place % 2, my_side()
    size = give_ref.shape[3]
    steps = 4
    size_q = factor_ref.shape[1] // steps
    factor_copies, query_copies = [], []
    for i in range(steps):
        cols = slice(i * size_q, (i + 1) * size_q)
        factor_copies.append(
            pltpu.make_async_copy(factor_hbm.at[:, cols], factor_ref.at[:, cols], sems.at[0, i])
        )
        query_copies.append(
            pltpu.make_async_copy(queries_hbm.at[:, cols], queries_ref.at[:, cols], sems.at[1, i])
        )
        factor_copies[i].start()
        query_copies[i].start()
    block = jnp.zeros_like(block_ref)
    for j in range(2):
        for i in range(j * steps // 2, (j + 1) * steps // 2):
            factor_copies[i].wait()
            query_copies[i].wait()
        piece = factor_ref.shape[1] // 2
        cols = slice(j * piece, (j + 1) * piece)
        block += lax.dot_general(
            factor_ref[:, cols],
            queries_ref[:, cols],
            (((1,), (1,)), ((), ())),
            preferred_element_type=F32,
        )
    for whose, out_ref in ((1 - core, give_ref), (core, keep_ref)):
        for i, where in enumerate((chip, 1 - chip)):
            for j, part in enumerate((side, 1 - side)):
                start = ((where * 2 + whose) * 2 + part) * size
                out_ref[i, j] = factor_ref[:, span(start, size)]
    block_ref[...] = block
    tiled_ref[...] = jnp.broadcast_to(block.astype(tiled_ref.dtype)[None], tiled_ref.shape)


def near_row_body(
    pieces, features_hbm, cols_ref, give_ref, keep_ref, features_ref, sems
):
    core, side = lax.axis_index("feat") % 2, my_side()
    half, depth = give_ref.shape[0], cols_ref.shape[0]
    steps = sems.shape[0]
    size = 2 * half // steps
    first = (1 - core) * half
    cols = cols_ref[...]
    copies = []
    for i in range(steps):
        rows = span(lax.rem(first + i * size, 2 * half), size)
        copies.append(
            pltpu.make_async_copy(features_hbm.at[rows], features_ref.at[rows], sems.at[i])
        )
    ahead = 6
    for copy in copies[:ahead]:
        copy.start()
    size = 2 * half // pieces
    for i in range(pieces):
        for j in range(i * steps // pieces, (i + 1) * steps // pieces):
            copies[j].wait()
            if j + ahead < steps:
                copies[j + ahead].start()
        rows = span(lax.rem(first + i * size, 2 * half), size)
        block = features_ref[rows, span(side * depth, depth)]
        out_ref, j = (give_ref, i) if i < pieces // 2 else (keep_ref, i - pieces // 2)
        out_ref[j * size : (j + 1) * size, :] = jnp.dot(block, cols, preferred_element_type=F32)


def far_row_body(features_ref, cols_ref, near_give_ref, near_keep_ref, give_ref, keep_ref):
    core, side = lax.axis_index("feat") % 2, my_side()
    half, depth = give_ref.shape[0], cols_ref.shape[0]
    cols = cols_ref[...]
    for part, near_ref, out_ref in (
        (1 - core, near_give_ref, give_ref),
        (core, near_keep_ref, keep_ref),
    ):
        block = features_ref[span(part * half, half), span((1 - side) * depth, depth)]
        product = near_ref[...] + jnp.dot(block, cols, preferred_element_type=F32)
        out_ref[...] = product.astype(out_ref.dtype)


def gram_body(other, features_ref, mine_ref, other_ref, out_ref, rows_ref):
    core = lax.axis_index("feat") % 2
    side = 1 - my_side() if other else my_side()
    size = mine_ref.shape[0]
    piece = 512
    rows_ref[span(core * size, size), :] = mine_ref[...]
    rows_ref[span((1 - core) * size, size), :] = other_ref[...]
    rows = rows_ref[...].T
    depth = out_ref.shape[0]
    for i in range(depth // piece):
        cols = span(side * depth + i * piece, piece)
        total = jnp.dot(rows, features_ref[:, cols], preferred_element_type=F32)
        out_ref[i * piece : (i + 1) * piece, :] = total.T.astype(out_ref.dtype)


def residual_body(total_rows, block_ref, parts_ref, out_ref):
    gram = jnp.sum(parts_ref[...].astype(F32), axis=0)
    residual = (gram / total_rows + 0.1 * block_ref[...]).astype(out_ref.dtype)
    out_ref[...] = jnp.broadcast_to(residual[None], out_ref.shape)


def product_body(factor_ref, cols_ref, give_ref, keep_ref):
    size = give_ref.shape[0]
    product = jnp.dot(factor_ref[...], cols_ref[...], preferred_element_type=F32)
    give_ref[...] = product[:size]
    keep_ref[...] = product[size:]


def load_body(own, features_hbm, out_ref, sems):
    chip = lax.axis_index("feat") // 2
    rows, steps = out_ref.shape[0], sems.shape[0]
    first, size = (chip if own else 1 - chip) * rows, rows // steps
    copies = [
        pltpu.make_async_copy(
            features_hbm.at[span(first + i * size, size)],
            out_ref.at[pl.ds(i * size, size)],
            sems.at[i],
        )
        for i in range(steps)
    ]
    for copy in copies:
        copy.start()
    for copy in copies:
        copy.wait()


def load_rows(features, own):
    shape = (features.shape[0] // 2, features.shape[1])
    (rows,) = local_call(
        functools.partial(load_body, own),
        (features,),
        [(shape, BF16)],
        "load_own" if own else "load_far",
        [pltpu.SemaphoreType.DMA((8,))],
        outside=1,
        limit=46,
    )
    return rows


def score_body(own, features_ref, cols_ref, give_ref, keep_ref, *ordered_ref):
    core = lax.axis_index("feat") % 2
    size = give_ref.shape[0]
    if own:
        cols = cols_ref[...]
    else:
        half, side = features_ref.shape[1] // 2, my_side()
        for i, part in enumerate((side, 1 - side)):
            ordered_ref[0][span(part * half, half), :] = cols_ref[:, i].reshape(half, -1)
        cols = ordered_ref[0][...]
    for whose, out_ref in ((1 - core, give_ref), (core, keep_ref)):
        rows = features_ref[span(whose * size, size), :]
        out_ref[...] = jnp.dot(rows, cols, preferred_element_type=F32).astype(out_ref.dtype)


def on_device(features, queries, inverse_factor):
    factor = inverse_factor[0]
    width = lax.axis_size("wide")
    row_count, cols = features.shape
    depth = factor.shape[0]
    count = queries.shape[0]
    total_rows = row_count * width

    query_block, tiled, give, keep = local_call(
        precond_body,
        (factor, queries),
        [((depth, count), F32), ((width // 2, depth, count), BF16)] + [((2, 2, depth, cols // 2), BF16)] * 2,
        "precond",
        [
            pltpu.VMEM(factor.shape, BF16),
            pltpu.VMEM(queries.shape, BF16),
            pltpu.SemaphoreType.DMA((2, 4)),
        ],
        outside=2,
        limit=53,
        )
    query_cols = exchange_side(tiled.reshape(cols // 2, count))
    got = swap_core(give)
    piece = [[jnp.stack([got[i, j], keep[i, j]]) for j in range(2)] for i in range(2)]
    piece[0][1] = swap_side(piece[0][1])
    piece[1][0] = swap_chip(piece[1][0])
    piece[1][1] = swap_chip_and_side(piece[1][1])
    factor_cols = jnp.stack([jnp.stack(row, 1) for row in piece], 1)
    factor_cols = factor_cols.reshape(8 * depth, cols // 2)

    half = (row_count // 2, count)
    far_cols = swap_side(query_cols)
    give, keep, held = local_call(
        functools.partial(near_row_body, 8),
        (features, query_cols),
        [(half, F32), (half, F32), (features.shape, BF16)],
        "near_rows",
        [pltpu.SemaphoreType.DMA((16,))],
        outside=1,
        limit=43,
    )
    give, keep = local_call(
        far_row_body, (held, far_cols, give, keep), [(half, BF16), (half, F32)], "far_rows"
    )
    chip_sum = (keep + swap_core(give).astype(F32)).astype(BF16)
    mine = (chip_sum.astype(F32) + swap_chip(chip_sum).astype(F32)).astype(BF16)
    other = swap_core(mine)

    parts = []
    for far in (True, False):
        (part,) = local_call(
            functools.partial(gram_body, far),
            (held, mine, other),
            [((cols // 2, count), BF16 if far else F32)],
            "far_gram" if far else "own_gram",
            [pltpu.VMEM((row_count, count), BF16)],
        )
        parts.append(part)
    gram_part = (parts[1] + swap_side(parts[0]).astype(F32)).astype(BF16)
    gram_parts = exchange_side(gram_part).reshape(width // 2, depth, count)
    (residual,) = local_call(
        functools.partial(residual_body, total_rows),
        (query_block, gram_parts),
        [((width // 2, depth, count), BF16)],
        "residual",
    )
    residual_cols = exchange_side(residual.reshape(cols // 2, count))

    part = (4 * depth, count)
    give, keep = local_call(
        product_body, (factor_cols, residual_cols), [(part, F32), (part, F32)], "product"
    )
    product = keep + swap_core(give)
    product, source = lax.optimization_barrier((product, features))
    far_features = load_rows(source, False)
    product = product[: 2 * depth] + swap_chip(product[2 * depth :])
    start = jnp.concatenate([2.0 * query_block - product[:depth], -product[depth:]])
    start, far_features, source = lax.optimization_barrier((start, far_features, features))
    own_features = load_rows(source, True)
    corrected = (start + jnp.roll(swap_side(start), depth, 0)).astype(BF16)
    corrected, own_features = lax.optimization_barrier((corrected, own_features))
    corrected_cols = exchange_side(jnp.tile(corrected, (width // 2, 1)))
    corrected_cols = corrected_cols.reshape(width // 2, 2, depth, count)

    quarter = (row_count // 4, count)
    give, keep, corrected_cols = local_call(
        functools.partial(score_body, False),
        (far_features, corrected_cols),
        [(quarter, BF16), (quarter, F32), ((cols, count), BF16)],
        "far_scores",
    )
    far = keep + swap_core(give).astype(F32)
    give, keep = local_call(
        functools.partial(score_body, True),
        (own_features, corrected_cols),
        [(quarter, BF16), (quarter, F32)],
        "own_scores",
    )
    own = keep + swap_core(give).astype(F32)
    return own + swap_chip(far.astype(BF16)).astype(F32)


def solution(mesh):
    in_specs = (P("wide", "feat"), P(), P("feat", "wide", None))
    out_specs = P(("wide", "feat"), None)
    return jax.shard_map(
        on_device, mesh=mesh, in_specs=in_specs, out_specs=out_specs, check_vma=False
    )
```

```python
import functools
import jax
import jax.numpy as jnp
from jax import lax
from jax.experimental import pallas as pl
from jax.experimental.pallas import tpu as pltpu
from jax.sharding import PartitionSpec as P

CORE_SWAP = [(0, 1), (1, 0), (2, 3), (3, 2)]
CHIP_SWAP = [(0, 2), (2, 0), (1, 3), (3, 1)]
F32, BF16 = jnp.float32, jnp.bfloat16
IN_VMEM = pl.BlockSpec(memory_space=pltpu.VMEM)


def swap_core(block):
    return lax.ppermute(block, "feat", CORE_SWAP)


def swap_chip(block):
    return lax.ppermute(block, "feat", CHIP_SWAP)


def swap_side(block):
    width = lax.axis_size("wide")
    return lax.ppermute(block, "wide", [(i, (i + width // 2) % width) for i in range(width)])


def swap_chip_and_side(block):
    width = lax.axis_size("wide")
    pairs = [
        (i * 4 + j, (i + width // 2) % width * 4 + k) for i in range(width) for j, k in CHIP_SWAP
    ]
    return lax.ppermute(block, ("wide", "feat"), pairs)


def exchange_side(blocks):
    half = lax.axis_size("wide") // 2
    sides = [list(range(half)), list(range(half, 2 * half))]
    return lax.all_to_all(blocks, "wide", 0, 0, tiled=True, axis_index_groups=sides)


def my_side():
    return lax.axis_index("wide") // (lax.axis_size("wide") // 2)


def local_call(body, operands, shapes, name, scratch=(), outside=0, limit=8):
    anywhere = pl.BlockSpec(memory_space=pl.ANY)
    return pl.pallas_call(
        body,
        in_specs=[anywhere] * outside + [IN_VMEM] * (len(operands) - outside),
        out_specs=[IN_VMEM] * len(shapes),
        out_shape=[jax.ShapeDtypeStruct(shape, dtype) for shape, dtype in shapes],
        scratch_shapes=list(scratch),
        compiler_params=pltpu.CompilerParams(vmem_limit_bytes=limit << 20),
        name=name,
    )(*operands)


def span(start, size):
    return pl.ds(pl.multiple_of(start, size), size)


def precond_body(
    factor_hbm, queries_hbm, block_ref, tiled_ref, give_ref, keep_ref, factor_ref, queries_ref, sems
):
    place = lax.axis_index("feat")
    chip, core, side = place // 2, place % 2, my_side()
    size = give_ref.shape[3]
    steps = 4
    size_q = factor_ref.shape[1] // steps
    factor_copies, query_copies = [], []
    for i in range(steps):
        cols = slice(i * size_q, (i + 1) * size_q)
        factor_copies.append(
            pltpu.make_async_copy(factor_hbm.at[:, cols], factor_ref.at[:, cols], sems.at[0, i])
        )
        query_copies.append(
            pltpu.make_async_copy(queries_hbm.at[:, cols], queries_ref.at[:, cols], sems.at[1, i])
        )
        factor_copies[i].start()
        query_copies[i].start()
    block = jnp.zeros_like(block_ref)
    for j in range(2):
        for i in range(j * steps // 2, (j + 1) * steps // 2):
            factor_copies[i].wait()
            query_copies[i].wait()
        piece = factor_ref.shape[1] // 2
        cols = slice(j * piece, (j + 1) * piece)
        block += lax.dot_general(
            factor_ref[:, cols],
            queries_ref[:, cols],
            (((1,), (1,)), ((), ())),
            preferred_element_type=F32,
        )
    for whose, out_ref in ((1 - core, give_ref), (core, keep_ref)):
        for i, where in enumerate((chip, 1 - chip)):
            for j, part in enumerate((side, 1 - side)):
                start = ((where * 2 + whose) * 2 + part) * size
                out_ref[i, j] = factor_ref[:, span(start, size)]
    block_ref[...] = block
    tiled_ref[...] = jnp.broadcast_to(block.astype(tiled_ref.dtype)[None], tiled_ref.shape)


def near_row_body(
    pieces, features_hbm, cols_ref, give_ref, keep_ref, features_ref, sems
):
    core, side = lax.axis_index("feat") % 2, my_side()
    half, depth = give_ref.shape[0], cols_ref.shape[0]
    steps = sems.shape[0]
    size = 2 * half // steps
    first = (1 - core) * half
    cols = cols_ref[...]
    copies = []
    for i in range(steps):
        rows = span(lax.rem(first + i * size, 2 * half), size)
        copies.append(
            pltpu.make_async_copy(features_hbm.at[rows], features_ref.at[rows], sems.at[i])
        )
    ahead = 6
    for copy in copies[:ahead]:
        copy.start()
    size = 2 * half // pieces
    for i in range(pieces):
        for j in range(i * steps // pieces, (i + 1) * steps // pieces):
            copies[j].wait()
            if j + ahead < steps:
                copies[j + ahead].start()
        rows = span(lax.rem(first + i * size, 2 * half), size)
        block = features_ref[rows, span(side * depth, depth)]
        out_ref, j = (give_ref, i) if i < pieces // 2 else (keep_ref, i - pieces // 2)
        out_ref[j * size : (j + 1) * size, :] = jnp.dot(block, cols, preferred_element_type=F32)


def far_row_body(
    piece, features_ref, cols_ref, near_give_ref, near_keep_ref, give_ref, keep_ref
):
    core, side = lax.axis_index("feat") % 2, my_side()
    size, depth, half = give_ref.shape[0], cols_ref.shape[0], near_give_ref.shape[0]
    cols = cols_ref[...]
    near = slice(piece * size, (piece + 1) * size)
    for part, near_ref, out_ref in (
        (1 - core, near_give_ref, give_ref),
        (core, near_keep_ref, keep_ref),
    ):
        rows = span(part * half + piece * size, size)
        block = features_ref[rows, span((1 - side) * depth, depth)]
        product = near_ref[near, :] + jnp.dot(block, cols, preferred_element_type=F32)
        out_ref[...] = product.astype(out_ref.dtype)


def gram_body(other, features_ref, *refs):
    *parts, out_ref, rows_ref = refs
    core = lax.axis_index("feat") % 2
    side = 1 - my_side() if other else my_side()
    size = parts[0].shape[0]
    half = size * len(parts) // 2
    for i, part_ref in enumerate(parts):
        whose = core if i % 2 == 0 else 1 - core
        rows_ref[span(whose * half + i // 2 * size, size), :] = part_ref[...]
    rows = rows_ref[...].T
    piece = 512
    depth = out_ref.shape[0]
    for i in range(depth // piece):
        cols = span(side * depth + i * piece, piece)
        total = jnp.dot(rows, features_ref[:, cols], preferred_element_type=F32)
        out_ref[i * piece : (i + 1) * piece, :] = total.T.astype(out_ref.dtype)


def residual_body(total_rows, block_ref, parts_ref, out_ref):
    gram = jnp.sum(parts_ref[...].astype(F32), axis=0)
    residual = (gram / total_rows + 0.1 * block_ref[...]).astype(out_ref.dtype)
    out_ref[...] = jnp.broadcast_to(residual[None], out_ref.shape)


def product_body(factor_ref, cols_ref, give_ref, keep_ref):
    size = give_ref.shape[0]
    product = jnp.dot(factor_ref[...], cols_ref[...], preferred_element_type=F32)
    give_ref[...] = product[:size]
    keep_ref[...] = product[size:]


def load_body(features_hbm, out_ref, sems):
    chip = lax.axis_index("feat") // 2
    rows, steps = out_ref.shape[0], sems.shape[0]
    size = rows // steps
    copies = [
        pltpu.make_async_copy(
            features_hbm.at[span((1 - chip) * rows + i * size, size)],
            out_ref.at[pl.ds(i * size, size)],
            sems.at[i],
        )
        for i in range(steps)
    ]
    for copy in copies:
        copy.start()
    for copy in copies:
        copy.wait()


def load_far_rows(features):
    shape = (features.shape[0] // 2, features.shape[1])
    (rows,) = local_call(
        load_body,
        (features,),
        [(shape, BF16)],
        "load_far",
        [pltpu.SemaphoreType.DMA((8,))],
        outside=1,
        limit=46,
    )
    return rows


def far_score_body(features_ref, cols_ref, give_ref, keep_ref, ordered_ref):
    core, side = lax.axis_index("feat") % 2, my_side()
    size, half = give_ref.shape[0], features_ref.shape[1] // 2
    for i, part in enumerate((side, 1 - side)):
        ordered_ref[span(part * half, half), :] = cols_ref[:, i].reshape(half, -1)
    cols = ordered_ref[...]
    for whose, out_ref in ((1 - core, give_ref), (core, keep_ref)):
        rows = features_ref[span(whose * size, size), :]
        out_ref[...] = jnp.dot(rows, cols, preferred_element_type=F32).astype(out_ref.dtype)


def own_score_body(features_hbm, cols_ref, give_ref, keep_ref, features_ref, sems):
    place = lax.axis_index("feat")
    chip, core = place // 2, place % 2
    half, steps = give_ref.shape[0], sems.shape[0]
    size = 2 * half // steps
    copies = []
    for i in range(steps):
        whose = 1 - core if i < steps // 2 else core
        start = (chip * 2 + whose) * half + i % (steps // 2) * size
        copies.append(
            pltpu.make_async_copy(
                features_hbm.at[span(start, size)],
                features_ref.at[pl.ds(i * size, size)],
                sems.at[i],
            )
        )
        copies[i].start()
    cols = cols_ref[...]
    size = half // 2
    for i in range(4):
        for copy in copies[i * steps // 4 : (i + 1) * steps // 4]:
            copy.wait()
        rows = features_ref[i * size : (i + 1) * size, :]
        out_ref = give_ref if i < 2 else keep_ref
        product = jnp.dot(rows, cols, preferred_element_type=F32)
        out_ref[i % 2 * size : (i % 2 + 1) * size, :] = product.astype(out_ref.dtype)


def own_columns(other_factor, near_factor):
    _, _, depth, cols = near_factor.shape
    pairs = [
        [jnp.stack([other_factor[i, j], near_factor[i, j]]) for j in range(2)] for i in range(2)
    ]
    pairs[0][1] = swap_side(pairs[0][1])
    pairs[1][0] = swap_chip(pairs[1][0])
    pairs[1][1] = swap_chip_and_side(pairs[1][1])
    return jnp.stack([jnp.stack(pair, 1) for pair in pairs], 1).reshape(8 * depth, cols)


def on_device(features, queries, inverse_factor):
    factor = inverse_factor[0]
    width = lax.axis_size("wide")
    row_count, cols = features.shape
    depth = factor.shape[0]
    count = queries.shape[0]
    total_rows = row_count * width

    query_block, tiled, far_factor, near_factor = local_call(
        precond_body,
        (factor, queries),
        [((depth, count), F32), ((width // 2, depth, count), BF16)] + [((2, 2, depth, cols // 2), BF16)] * 2,
        "precond",
        [
            pltpu.VMEM(factor.shape, BF16),
            pltpu.VMEM(queries.shape, BF16),
            pltpu.SemaphoreType.DMA((2, 4)),
        ],
        outside=2,
        limit=53,
        )
    query_cols = exchange_side(tiled.reshape(cols // 2, count))
    half = (row_count // 2, count)
    far_cols = swap_side(query_cols)
    give, keep, held = local_call(
        functools.partial(near_row_body, 8),
        (features, query_cols),
        [(half, F32), (half, F32), (features.shape, BF16)],
        "near_rows",
        [pltpu.SemaphoreType.DMA((16,))],
        outside=1,
        limit=43,
    )
    quarter = (row_count // 4, count)
    sums = []
    for i in range(2):
        part, kept = local_call(
            functools.partial(far_row_body, i),
            (held, far_cols, give, keep),
            [(quarter, BF16), (quarter, F32)],
            f"far_rows_{i}",
        )
        sums.append((kept, swap_core(part)))
    row_weights = []
    for kept, got in sums:
        chip_sum = (kept + got.astype(F32)).astype(BF16)
        mine = (chip_sum.astype(F32) + swap_chip(chip_sum).astype(F32)).astype(BF16)
        row_weights += [mine, swap_core(mine)]

    parts = []
    for far in (True, False):
        (part,) = local_call(
            functools.partial(gram_body, far),
            (held, *row_weights),
            [((cols // 2, count), BF16 if far else F32)],
            "far_gram" if far else "own_gram",
            [pltpu.VMEM((row_count, count), BF16)],
        )
        parts.append(part)
    gram_part = (parts[1] + swap_side(parts[0]).astype(F32)).astype(BF16)
    other_factor = swap_core(far_factor)
    gram_part, other_factor = lax.optimization_barrier((gram_part, other_factor))
    gram_parts = exchange_side(gram_part).reshape(width // 2, depth, count)
    (residual,) = local_call(
        functools.partial(residual_body, total_rows),
        (query_block, gram_parts),
        [((width // 2, depth, count), BF16)],
        "residual",
    )
    factor_cols = own_columns(other_factor, near_factor)
    residual_cols = exchange_side(residual.reshape(cols // 2, count))

    part = (4 * depth, count)
    give, keep = local_call(
        product_body, (factor_cols, residual_cols), [(part, F32), (part, F32)], "product"
    )
    product = keep + swap_core(give)
    product, source = lax.optimization_barrier((product, features))
    own, far = product[: 2 * depth], -product[2 * depth :]
    own = jnp.concatenate([2.0 * query_block - own[:depth], -own[depth:]])
    crossed = swap_side(own) + swap_chip_and_side(far)
    corrected = own + swap_chip(far) + jnp.roll(crossed, depth, 0)
    far_features = load_far_rows(source)
    corrected, far_features = lax.optimization_barrier((corrected.astype(BF16), far_features))
    corrected_cols = exchange_side(jnp.tile(corrected, (width // 2, 1)))
    corrected_cols = corrected_cols.reshape(width // 2, 2, depth, count)

    quarter = (row_count // 4, count)
    give, keep, corrected_cols = local_call(
        far_score_body,
        (far_features, corrected_cols),
        [(quarter, BF16), (quarter, F32), ((cols, count), BF16)],
        "far_scores",
    )
    far = (keep + swap_core(give).astype(F32)).astype(BF16)
    far, corrected_cols, source = lax.optimization_barrier((far, corrected_cols, features))
    give, keep = local_call(
        own_score_body,
        (source, corrected_cols),
        [(quarter, BF16), (quarter, F32)],
        "own_scores",
        [pltpu.VMEM((row_count // 2, cols), BF16), pltpu.SemaphoreType.DMA((8,))],
        outside=1,
        limit=46,
    )
    size = row_count // 8
    got = jnp.concatenate([swap_core(give[:size]), swap_core(give[size:])])
    return keep + got.astype(F32) + swap_chip(far).astype(F32)


def solution(mesh):
    in_specs = (P("wide", "feat"), P(), P("feat", "wide", None))
    out_specs = P(("wide", "feat"), None)
    return jax.shard_map(
        on_device, mesh=mesh, in_specs=in_specs, out_specs=out_specs, check_vma=False
    )
```

```python
import functools
import jax
import jax.numpy as jnp
from jax import lax
from jax.experimental import pallas as pl
from jax.experimental.pallas import tpu as pltpu
from jax.sharding import PartitionSpec as P

CORE_SWAP = [(0, 1), (1, 0), (2, 3), (3, 2)]
CHIP_SWAP = [(0, 2), (2, 0), (1, 3), (3, 1)]
F32, BF16 = jnp.float32, jnp.bfloat16
IN_VMEM = pl.BlockSpec(memory_space=pltpu.VMEM)


def swap_core(block):
    return lax.ppermute(block, "feat", CORE_SWAP)


def swap_chip(block):
    return lax.ppermute(block, "feat", CHIP_SWAP)


def swap_side(block):
    width = lax.axis_size("wide")
    return lax.ppermute(block, "wide", [(i, (i + width // 2) % width) for i in range(width)])


def swap_chip_and_side(block):
    width = lax.axis_size("wide")
    pairs = [
        (i * 4 + j, (i + width // 2) % width * 4 + k) for i in range(width) for j, k in CHIP_SWAP
    ]
    return lax.ppermute(block, ("wide", "feat"), pairs)


def exchange_side(blocks):
    half = lax.axis_size("wide") // 2
    sides = [list(range(half)), list(range(half, 2 * half))]
    return lax.all_to_all(blocks, "wide", 0, 0, tiled=True, axis_index_groups=sides)


def my_side():
    return lax.axis_index("wide") // (lax.axis_size("wide") // 2)


def local_call(body, operands, shapes, name, scratch=(), outside=0, limit=8):
    anywhere = pl.BlockSpec(memory_space=pl.ANY)
    return pl.pallas_call(
        body,
        in_specs=[anywhere] * outside + [IN_VMEM] * (len(operands) - outside),
        out_specs=[IN_VMEM] * len(shapes),
        out_shape=[jax.ShapeDtypeStruct(shape, dtype) for shape, dtype in shapes],
        scratch_shapes=list(scratch),
        compiler_params=pltpu.CompilerParams(vmem_limit_bytes=limit << 20),
        name=name,
    )(*operands)


def span(start, size):
    return pl.ds(pl.multiple_of(start, size), size)


def precond_body(
    factor_hbm, queries_hbm, block_ref, tiled_ref, give_ref, keep_ref, factor_ref, queries_ref, sems
):
    place = lax.axis_index("feat")
    chip, core, side = place // 2, place % 2, my_side()
    size = give_ref.shape[3]
    steps = 4
    size_q = factor_ref.shape[1] // steps
    factor_copies, query_copies = [], []
    for i in range(steps):
        cols = slice(i * size_q, (i + 1) * size_q)
        factor_copies.append(
            pltpu.make_async_copy(factor_hbm.at[:, cols], factor_ref.at[:, cols], sems.at[0, i])
        )
        query_copies.append(
            pltpu.make_async_copy(queries_hbm.at[:, cols], queries_ref.at[:, cols], sems.at[1, i])
        )
        factor_copies[i].start()
        query_copies[i].start()
    block = jnp.zeros_like(block_ref)
    for j in range(2):
        for i in range(j * steps // 2, (j + 1) * steps // 2):
            factor_copies[i].wait()
            query_copies[i].wait()
        piece = factor_ref.shape[1] // 2
        cols = slice(j * piece, (j + 1) * piece)
        block += lax.dot_general(
            factor_ref[:, cols],
            queries_ref[:, cols],
            (((1,), (1,)), ((), ())),
            preferred_element_type=F32,
        )
    for whose, out_ref in ((1 - core, give_ref), (core, keep_ref)):
        for i, where in enumerate((chip, 1 - chip)):
            for j, part in enumerate((side, 1 - side)):
                start = ((where * 2 + whose) * 2 + part) * size
                out_ref[i, j] = factor_ref[:, span(start, size)]
    block_ref[...] = block
    tiled_ref[...] = jnp.broadcast_to(block.astype(tiled_ref.dtype)[None], tiled_ref.shape)


def near_row_body(
    pieces, features_hbm, cols_ref, give_ref, keep_ref, features_ref, sems
):
    core, side = lax.axis_index("feat") % 2, my_side()
    half, depth = give_ref.shape[0], cols_ref.shape[0]
    steps = sems.shape[0]
    size = 2 * half // steps
    first = (1 - core) * half
    cols = cols_ref[...]
    copies = []
    for i in range(steps):
        rows = span(lax.rem(first + i * size, 2 * half), size)
        copies.append(
            pltpu.make_async_copy(features_hbm.at[rows], features_ref.at[rows], sems.at[i])
        )
    ahead = 6
    for copy in copies[:ahead]:
        copy.start()
    size = 2 * half // pieces
    for i in range(pieces):
        for j in range(i * steps // pieces, (i + 1) * steps // pieces):
            copies[j].wait()
            if j + ahead < steps:
                copies[j + ahead].start()
        rows = span(lax.rem(first + i * size, 2 * half), size)
        block = features_ref[rows, span(side * depth, depth)]
        out_ref, j = (give_ref, i) if i < pieces // 2 else (keep_ref, i - pieces // 2)
        out_ref[j * size : (j + 1) * size, :] = jnp.dot(block, cols, preferred_element_type=F32)


def far_row_body(
    piece, features_ref, cols_ref, near_give_ref, near_keep_ref, give_ref, keep_ref
):
    core, side = lax.axis_index("feat") % 2, my_side()
    size, depth, half = give_ref.shape[0], cols_ref.shape[0], near_give_ref.shape[0]
    cols = cols_ref[...]
    near = slice(piece * size, (piece + 1) * size)
    for part, near_ref, out_ref in (
        (1 - core, near_give_ref, give_ref),
        (core, near_keep_ref, keep_ref),
    ):
        rows = span(part * half + piece * size, size)
        block = features_ref[rows, span((1 - side) * depth, depth)]
        product = near_ref[near, :] + jnp.dot(block, cols, preferred_element_type=F32)
        out_ref[...] = product.astype(out_ref.dtype)


def gram_body(chunk, other, features_ref, mine_ref, other_ref, *refs):
    *before, out_ref, rows_ref = refs
    core = lax.axis_index("feat") % 2
    side = 1 - my_side() if other else my_side()
    size = mine_ref.shape[0]
    half = features_ref.shape[0] // 2
    rows_ref[span(core * size, size), :] = mine_ref[...]
    rows_ref[span((1 - core) * size, size), :] = other_ref[...]
    rows = rows_ref[...].T
    piece = 512
    depth = out_ref.shape[0]
    for i in range(depth // piece):
        cols = span(side * depth + i * piece, piece)
        total = sum(
            jnp.dot(
                rows[:, j * size : (j + 1) * size],
                features_ref[j * half + chunk * size : j * half + (chunk + 1) * size, cols],
                preferred_element_type=F32,
            )
            for j in range(2)
        )
        where = slice(i * piece, (i + 1) * piece)
        total = total.T
        if before:
            total += before[0][where, :]
        out_ref[where, :] = total.astype(out_ref.dtype)


def residual_body(total_rows, block_ref, parts_ref, out_ref):
    gram = jnp.sum(parts_ref[...].astype(F32), axis=0)
    residual = (gram / total_rows + 0.1 * block_ref[...]).astype(out_ref.dtype)
    out_ref[...] = jnp.broadcast_to(residual[None], out_ref.shape)


def product_body(factor_ref, cols_ref, give_ref, keep_ref):
    size = give_ref.shape[0]
    product = jnp.dot(factor_ref[...], cols_ref[...], preferred_element_type=F32)
    give_ref[...] = product[:size]
    keep_ref[...] = product[size:]


def load_body(features_hbm, out_ref, sems):
    place = lax.axis_index("feat")
    chip, core = place // 2, place % 2
    quarter = features_hbm.shape[0] // 4
    steps = sems.shape[0] // 3
    size = quarter // steps
    copies = []
    for i, part in enumerate((2 - 2 * chip, 3 - 2 * chip, 2 * chip + 1 - core)):
        for j in range(steps):
            copies.append(
                pltpu.make_async_copy(
                    features_hbm.at[span(part * quarter + j * size, size)],
                    out_ref.at[pl.ds(i * quarter + j * size, size)],
                    sems.at[i * steps + j],
                )
            )
    for copy in copies:
        copy.start()
    for copy in copies:
        copy.wait()


def load_rows(features):
    (rows,) = local_call(
        load_body,
        (features,),
        [((features.shape[0] // 4 * 3, features.shape[1]), BF16)],
        "load",
        [pltpu.SemaphoreType.DMA((12,))],
        outside=1,
        limit=44,
    )
    return rows


def far_score_body(features_ref, cols_ref, give_ref, keep_ref, ordered_ref):
    core, side = lax.axis_index("feat") % 2, my_side()
    size, half = give_ref.shape[0], features_ref.shape[1] // 2
    for i, part in enumerate((side, 1 - side)):
        ordered_ref[span(part * half, half), :] = cols_ref[:, i].reshape(half, -1)
    cols = ordered_ref[...]
    for whose, out_ref in ((1 - core, give_ref), (core, keep_ref)):
        rows = features_ref[span(whose * size, size), :]
        out_ref[...] = jnp.dot(rows, cols, preferred_element_type=F32).astype(out_ref.dtype)


def give_score_body(features_ref, cols_ref, out_ref):
    rows = out_ref.shape[0]
    product = jnp.dot(features_ref[2 * rows :, :], cols_ref[...], preferred_element_type=F32)
    out_ref[...] = product.astype(out_ref.dtype)


def keep_score_body(features_hbm, cols_ref, out_ref, features_ref, sems):
    place = lax.axis_index("feat")
    rows, steps = out_ref.shape[0], sems.shape[0]
    size = rows // steps
    copies = []
    for i in range(steps):
        copies.append(
            pltpu.make_async_copy(
                features_hbm.at[span(place * rows + i * size, size)],
                features_ref.at[pl.ds(i * size, size)],
                sems.at[i],
            )
        )
        copies[i].start()
    cols = cols_ref[...]
    size = rows // 2
    for i in range(2):
        for copy in copies[i * steps // 2 : (i + 1) * steps // 2]:
            copy.wait()
        piece = slice(i * size, (i + 1) * size)
        out_ref[piece, :] = jnp.dot(features_ref[piece, :], cols, preferred_element_type=F32)


def own_columns(other_factor, near_factor):
    _, _, depth, cols = near_factor.shape
    pairs = [
        [jnp.stack([other_factor[i, j], near_factor[i, j]]) for j in range(2)] for i in range(2)
    ]
    pairs[0][1] = swap_side(pairs[0][1])
    pairs[1][0] = swap_chip(pairs[1][0])
    pairs[1][1] = swap_chip_and_side(pairs[1][1])
    return jnp.stack([jnp.stack(pair, 1) for pair in pairs], 1).reshape(8 * depth, cols)


def on_device(features, queries, inverse_factor):
    factor = inverse_factor[0]
    width = lax.axis_size("wide")
    row_count, cols = features.shape
    depth = factor.shape[0]
    count = queries.shape[0]
    total_rows = row_count * width

    query_block, tiled, far_factor, near_factor = local_call(
        precond_body,
        (factor, queries),
        [((depth, count), F32), ((width // 2, depth, count), BF16)] + [((2, 2, depth, cols // 2), BF16)] * 2,
        "precond",
        [
            pltpu.VMEM(factor.shape, BF16),
            pltpu.VMEM(queries.shape, BF16),
            pltpu.SemaphoreType.DMA((2, 4)),
        ],
        outside=2,
        limit=53,
        )
    query_cols = exchange_side(tiled.reshape(cols // 2, count))
    half = (row_count // 2, count)
    far_cols = swap_side(query_cols)
    give, keep, held = local_call(
        functools.partial(near_row_body, 8),
        (features, query_cols),
        [(half, F32), (half, F32), (features.shape, BF16)],
        "near_rows",
        [pltpu.SemaphoreType.DMA((16,))],
        outside=1,
        limit=43,
    )
    quarter = (row_count // 4, count)
    sums = []
    for i in range(2):
        part, kept = local_call(
            functools.partial(far_row_body, i),
            (held, far_cols, give, keep),
            [(quarter, BF16), (quarter, F32)],
            f"far_rows_{i}",
        )
        sums.append((kept, swap_core(part)))
    row_weights = []
    for kept, got in sums:
        chip_sum = (kept + got.astype(F32)).astype(BF16)
        mine = (chip_sum.astype(F32) + swap_chip(chip_sum).astype(F32)).astype(BF16)
        row_weights += [mine, swap_core(mine)]

    parts = [None, None]
    for i in (1, 1 - 1):
        for j, far in enumerate((True, False)):
            last = i != 1
            before = () if not last else (parts[j],)
            (parts[j],) = local_call(
                functools.partial(gram_body, i, far),
                (held, *row_weights[2 * i : 2 * i + 2], *before),
                [((cols // 2, count), BF16 if far and last else F32)],
                f"far_gram_{i}" if far else f"own_gram_{i}",
                [pltpu.VMEM((row_count // 2, count), BF16)],
            )
    gram_part = (parts[1] + swap_side(parts[0]).astype(F32)).astype(BF16)
    other_factor = swap_core(far_factor)
    gram_part, other_factor = lax.optimization_barrier((gram_part, other_factor))
    gram_parts = exchange_side(gram_part).reshape(width // 2, depth, count)
    (residual,) = local_call(
        functools.partial(residual_body, total_rows),
        (query_block, gram_parts),
        [((width // 2, depth, count), BF16)],
        "residual",
    )
    factor_cols = own_columns(other_factor, near_factor)
    residual_cols = exchange_side(residual.reshape(cols // 2, count))

    part = (4 * depth, count)
    give, keep = local_call(
        product_body, (factor_cols, residual_cols), [(part, F32), (part, F32)], "product"
    )
    product = keep + swap_core(give)
    product, source = lax.optimization_barrier((product, features))
    own, far = product[: 2 * depth], -product[2 * depth :]
    own = jnp.concatenate([2.0 * query_block - own[:depth], -own[depth:]])
    crossed = swap_side(own) + swap_chip_and_side(far)
    corrected = own + swap_chip(far) + jnp.roll(crossed, depth, 0)
    loaded = load_rows(source)
    corrected, loaded = lax.optimization_barrier((corrected.astype(BF16), loaded))
    corrected_cols = exchange_side(jnp.tile(corrected, (width // 2, 1)))
    corrected_cols = corrected_cols.reshape(width // 2, 2, depth, count)

    quarter = (row_count // 4, count)
    give, keep, corrected_cols = local_call(
        far_score_body,
        (loaded, corrected_cols),
        [(quarter, BF16), (quarter, F32), ((cols, count), BF16)],
        "far_scores",
    )
    far = (keep + swap_core(give).astype(F32)).astype(BF16)
    (give,) = local_call(
        give_score_body, (loaded, corrected_cols), [(quarter, BF16)], "give_scores"
    )
    far, corrected_cols, source = lax.optimization_barrier((far, corrected_cols, features))
    (keep,) = local_call(
        keep_score_body,
        (source, corrected_cols),
        [(quarter, F32)],
        "keep_scores",
        [pltpu.VMEM((row_count // 4, cols), BF16), pltpu.SemaphoreType.DMA((4,))],
        outside=1,
        limit=46,
    )
    size = row_count // 8
    got = jnp.concatenate([swap_core(give[:size]), swap_core(give[size:])])
    return keep + got.astype(F32) + swap_chip(far).astype(F32)


def solution(mesh):
    in_specs = (P("wide", "feat"), P(), P("feat", "wide", None))
    out_specs = P(("wide", "feat"), None)
    return jax.shard_map(
        on_device, mesh=mesh, in_specs=in_specs, out_specs=out_specs, check_vma=False
    )
```

```python
import functools
import jax
import jax.numpy as jnp
from jax import lax
from jax.experimental import pallas as pl
from jax.experimental.pallas import tpu as pltpu
from jax.sharding import PartitionSpec as P

CORE_SWAP = [(0, 1), (1, 0), (2, 3), (3, 2)]
CHIP_SWAP = [(0, 2), (2, 0), (1, 3), (3, 1)]
F32, BF16 = jnp.float32, jnp.bfloat16
IN_VMEM = pl.BlockSpec(memory_space=pltpu.VMEM)


def swap_core(block):
    return lax.ppermute(block, "feat", CORE_SWAP)


def swap_chip(block):
    return lax.ppermute(block, "feat", CHIP_SWAP)


def swap_side(block):
    width = lax.axis_size("wide")
    return lax.ppermute(block, "wide", [(i, (i + width // 2) % width) for i in range(width)])


def swap_chip_and_side(block):
    width = lax.axis_size("wide")
    pairs = [
        (i * 4 + j, (i + width // 2) % width * 4 + k) for i in range(width) for j, k in CHIP_SWAP
    ]
    return lax.ppermute(block, ("wide", "feat"), pairs)


def exchange_side(blocks):
    half = lax.axis_size("wide") // 2
    sides = [list(range(half)), list(range(half, 2 * half))]
    return lax.all_to_all(blocks, "wide", 0, 0, tiled=True, axis_index_groups=sides)


def my_side():
    return lax.axis_index("wide") // (lax.axis_size("wide") // 2)


def local_call(body, operands, shapes, name, scratch=(), outside=0, limit=8):
    anywhere = pl.BlockSpec(memory_space=pl.ANY)
    return pl.pallas_call(
        body,
        in_specs=[anywhere] * outside + [IN_VMEM] * (len(operands) - outside),
        out_specs=[IN_VMEM] * len(shapes),
        out_shape=[jax.ShapeDtypeStruct(shape, dtype) for shape, dtype in shapes],
        scratch_shapes=list(scratch),
        compiler_params=pltpu.CompilerParams(vmem_limit_bytes=limit << 20),
        name=name,
    )(*operands)


def span(start, size):
    return pl.ds(pl.multiple_of(start, size), size)


def precond_body(
    factor_hbm, queries_hbm, block_ref, tiled_ref, give_ref, keep_ref, factor_ref, queries_ref, sems
):
    place = lax.axis_index("feat")
    chip, core, side = place // 2, place % 2, my_side()
    size = give_ref.shape[3]
    steps = 4
    size_q = factor_ref.shape[1] // steps
    factor_copies, query_copies = [], []
    for i in range(steps):
        cols = slice(i * size_q, (i + 1) * size_q)
        factor_copies.append(
            pltpu.make_async_copy(factor_hbm.at[:, cols], factor_ref.at[:, cols], sems.at[0, i])
        )
        query_copies.append(
            pltpu.make_async_copy(queries_hbm.at[:, cols], queries_ref.at[:, cols], sems.at[1, i])
        )
        factor_copies[i].start()
        query_copies[i].start()
    block = jnp.zeros_like(block_ref)
    for j in range(2):
        for i in range(j * steps // 2, (j + 1) * steps // 2):
            factor_copies[i].wait()
            query_copies[i].wait()
        piece = factor_ref.shape[1] // 2
        cols = slice(j * piece, (j + 1) * piece)
        block += lax.dot_general(
            factor_ref[:, cols],
            queries_ref[:, cols],
            (((1,), (1,)), ((), ())),
            preferred_element_type=F32,
        )
    for whose, out_ref in ((1 - core, give_ref), (core, keep_ref)):
        for i, where in enumerate((chip, 1 - chip)):
            for j, part in enumerate((side, 1 - side)):
                start = ((where * 2 + whose) * 2 + part) * size
                out_ref[i, j] = factor_ref[:, span(start, size)]
    block_ref[...] = block
    tiled_ref[...] = jnp.broadcast_to(block.astype(tiled_ref.dtype)[None], tiled_ref.shape)


def near_row_body(
    pieces, features_hbm, cols_ref, give_ref, keep_ref, features_ref, sems
):
    core, side = lax.axis_index("feat") % 2, my_side()
    half, depth = give_ref.shape[0], cols_ref.shape[0]
    steps = sems.shape[0]
    size = 2 * half // steps
    first = (1 - core) * half
    cols = cols_ref[...]
    copies = []
    for i in range(steps):
        rows = span(lax.rem(first + i * size, 2 * half), size)
        copies.append(
            pltpu.make_async_copy(features_hbm.at[rows], features_ref.at[rows], sems.at[i])
        )
    ahead = 6
    for copy in copies[:ahead]:
        copy.start()
    size = 2 * half // pieces
    for i in range(pieces):
        for j in range(i * steps // pieces, (i + 1) * steps // pieces):
            copies[j].wait()
            if j + ahead < steps:
                copies[j + ahead].start()
        rows = span(lax.rem(first + i * size, 2 * half), size)
        block = features_ref[rows, span(side * depth, depth)]
        out_ref, j = (give_ref, i) if i < pieces // 2 else (keep_ref, i - pieces // 2)
        out_ref[j * size : (j + 1) * size, :] = jnp.dot(block, cols, preferred_element_type=F32)


def far_row_body(
    piece, features_ref, cols_ref, near_give_ref, near_keep_ref, give_ref, keep_ref
):
    core, side = lax.axis_index("feat") % 2, my_side()
    size, depth, half = give_ref.shape[0], cols_ref.shape[0], near_give_ref.shape[0]
    cols = cols_ref[...]
    near = slice(piece * size, (piece + 1) * size)
    for part, near_ref, out_ref in (
        (1 - core, near_give_ref, give_ref),
        (core, near_keep_ref, keep_ref),
    ):
        rows = span(part * half + piece * size, size)
        block = features_ref[rows, span((1 - side) * depth, depth)]
        product = near_ref[near, :] + jnp.dot(block, cols, preferred_element_type=F32)
        out_ref[...] = product.astype(out_ref.dtype)


def gram_body(chunk, other, features_ref, mine_ref, other_ref, *refs):
    *before, out_ref, rows_ref = refs
    core = lax.axis_index("feat") % 2
    side = 1 - my_side() if other else my_side()
    size = mine_ref.shape[0]
    half = features_ref.shape[0] // 2
    rows_ref[span(core * size, size), :] = mine_ref[...]
    rows_ref[span((1 - core) * size, size), :] = other_ref[...]
    rows = rows_ref[...].T
    piece = 512
    depth = out_ref.shape[0]
    for i in range(depth // piece):
        cols = span(side * depth + i * piece, piece)
        total = sum(
            jnp.dot(
                rows[:, j * size : (j + 1) * size],
                features_ref[j * half + chunk * size : j * half + (chunk + 1) * size, cols],
                preferred_element_type=F32,
            )
            for j in range(2)
        )
        where = slice(i * piece, (i + 1) * piece)
        total = total.T
        if before:
            total += before[0][where, :]
        out_ref[where, :] = total.astype(out_ref.dtype)


def residual_body(total_rows, block_ref, parts_ref, out_ref):
    gram = jnp.sum(parts_ref[...].astype(F32), axis=0)
    residual = (gram / total_rows + 0.1 * block_ref[...]).astype(out_ref.dtype)
    out_ref[...] = jnp.broadcast_to(residual[None], out_ref.shape)


def product_body(factor_ref, cols_ref, give_ref, keep_ref):
    size = give_ref.shape[0]
    product = jnp.dot(factor_ref[...], cols_ref[...], preferred_element_type=F32)
    give_ref[...] = product[:size]
    keep_ref[...] = product[size:]


def load_body(features_hbm, out_ref, sems):
    place = lax.axis_index("feat")
    chip, core = place // 2, place % 2
    quarter = features_hbm.shape[0] // 4
    steps = sems.shape[0] // 3
    size = quarter // steps
    copies = []
    for i, part in enumerate((2 - 2 * chip, 3 - 2 * chip, 2 * chip + 1 - core)):
        for j in range(steps):
            copies.append(
                pltpu.make_async_copy(
                    features_hbm.at[span(part * quarter + j * size, size)],
                    out_ref.at[pl.ds(i * quarter + j * size, size)],
                    sems.at[i * steps + j],
                )
            )
    for copy in copies:
        copy.start()
    for copy in copies:
        copy.wait()


def load_rows(features):
    (rows,) = local_call(
        load_body,
        (features,),
        [((features.shape[0] // 4 * 3, features.shape[1]), BF16)],
        "load",
        [pltpu.SemaphoreType.DMA((12,))],
        outside=1,
        limit=44,
    )
    return rows


def far_score_body(features_ref, cols_ref, give_ref, keep_ref, ordered_ref):
    core, side = lax.axis_index("feat") % 2, my_side()
    size, half = give_ref.shape[0], features_ref.shape[1] // 2
    for i, part in enumerate((side, 1 - side)):
        ordered_ref[span(part * half, half), :] = cols_ref[:, i].reshape(half, -1)
    cols = ordered_ref[...]
    for whose, out_ref in ((1 - core, give_ref), (core, keep_ref)):
        rows = features_ref[span(whose * size, size), :]
        out_ref[...] = jnp.dot(rows, cols, preferred_element_type=F32).astype(out_ref.dtype)


def give_score_body(features_ref, cols_ref, out_ref):
    rows = out_ref.shape[0]
    product = jnp.dot(features_ref[2 * rows :, :], cols_ref[...], preferred_element_type=F32)
    out_ref[...] = product.astype(out_ref.dtype)


def keep_score_body(features_hbm, cols_ref, out_ref, features_ref, sems):
    place = lax.axis_index("feat")
    rows, steps = out_ref.shape[0], sems.shape[0]
    size = rows // steps
    copies = []
    for i in range(steps):
        copies.append(
            pltpu.make_async_copy(
                features_hbm.at[span(place * rows + i * size, size)],
                features_ref.at[pl.ds(i * size, size)],
                sems.at[i],
            )
        )
        copies[i].start()
    cols = cols_ref[...]
    size = rows // 2
    for i in range(2):
        for copy in copies[i * steps // 2 : (i + 1) * steps // 2]:
            copy.wait()
        piece = slice(i * size, (i + 1) * size)
        out_ref[piece, :] = jnp.dot(features_ref[piece, :], cols, preferred_element_type=F32)


def own_columns(other_factor, near_factor):
    _, _, depth, cols = near_factor.shape
    pairs = [
        [jnp.stack([other_factor[i, j], near_factor[i, j]]) for j in range(2)] for i in range(2)
    ]
    pairs[0][1] = swap_side(pairs[0][1])
    pairs[1][0] = swap_chip(pairs[1][0])
    pairs[1][1] = swap_chip_and_side(pairs[1][1])
    return jnp.stack([jnp.stack(pair, 1) for pair in pairs], 1).reshape(8 * depth, cols)


def on_device(features, queries, inverse_factor):
    factor = inverse_factor[0]
    width = lax.axis_size("wide")
    row_count, cols = features.shape
    depth = factor.shape[0]
    count = queries.shape[0]
    total_rows = row_count * width

    query_block, tiled, far_factor, near_factor = local_call(
        precond_body,
        (factor, queries),
        [((depth, count), F32), ((width // 2, depth, count), BF16)] + [((2, 2, depth, cols // 2), BF16)] * 2,
        "precond",
        [
            pltpu.VMEM(factor.shape, BF16),
            pltpu.VMEM(queries.shape, BF16),
            pltpu.SemaphoreType.DMA((2, 4)),
        ],
        outside=2,
        limit=53,
        )
    query_cols = exchange_side(tiled.reshape(cols // 2, count))
    half = (row_count // 2, count)
    far_cols = swap_side(query_cols)
    give, keep, held = local_call(
        functools.partial(near_row_body, 8),
        (features, query_cols),
        [(half, F32), (half, F32), (features.shape, BF16)],
        "near_rows",
        [pltpu.SemaphoreType.DMA((16,))],
        outside=1,
        limit=43,
    )
    quarter = (row_count // 4, count)
    sums = []
    for i in range(2):
        part, kept = local_call(
            functools.partial(far_row_body, i),
            (held, far_cols, give, keep),
            [(quarter, BF16), (quarter, F32)],
            f"far_rows_{i}",
        )
        sums.append((kept, swap_core(part)))
    row_weights = []
    for kept, got in sums:
        chip_sum = (kept + got.astype(F32)).astype(BF16)
        mine = (chip_sum.astype(F32) + swap_chip(chip_sum).astype(F32)).astype(BF16)
        row_weights += [mine, swap_core(mine)]

    parts = [None, None]
    for i in (1, 1 - 1):
        for j, far in enumerate((True, False)):
            last = i != 1
            before = () if not last else (parts[j],)
            (parts[j],) = local_call(
                functools.partial(gram_body, i, far),
                (held, *row_weights[2 * i : 2 * i + 2], *before),
                [((cols // 2, count), BF16 if far and last else F32)],
                f"far_gram_{i}" if far else f"own_gram_{i}",
                [pltpu.VMEM((row_count // 2, count), BF16)],
            )
    gram_part = (parts[1] + swap_side(parts[0]).astype(F32)).astype(BF16)
    other_factor = swap_core(far_factor)
    gram_part, other_factor = lax.optimization_barrier((gram_part, other_factor))
    gram_parts = exchange_side(gram_part).reshape(width // 2, depth, count)
    (residual,) = local_call(
        functools.partial(residual_body, total_rows),
        (query_block, gram_parts),
        [((width // 2, depth, count), BF16)],
        "residual",
    )
    factor_cols = own_columns(other_factor, near_factor)
    residual_cols = exchange_side(residual.reshape(cols // 2, count))

    part = (4 * depth, count)
    give, keep = local_call(
        product_body, (factor_cols, residual_cols), [(part, F32), (part, F32)], "product"
    )
    product = keep + swap_core(give)
    product, source = lax.optimization_barrier((product, features))
    own, far = product[: 2 * depth], -product[2 * depth :]
    own = jnp.concatenate([2.0 * query_block - own[:depth], -own[depth:]])
    near, far = own.astype(BF16), far.astype(BF16)
    crossed = swap_side(near).astype(F32) + swap_chip_and_side(far).astype(F32)
    corrected = own + swap_chip(far).astype(F32) + jnp.roll(crossed, depth, 0)
    loaded = load_rows(source)
    corrected, loaded = lax.optimization_barrier((corrected.astype(BF16), loaded))
    corrected_cols = exchange_side(jnp.tile(corrected, (width // 2, 1)))
    corrected_cols = corrected_cols.reshape(width // 2, 2, depth, count)

    quarter = (row_count // 4, count)
    give, keep, corrected_cols = local_call(
        far_score_body,
        (loaded, corrected_cols),
        [(quarter, BF16), (quarter, F32), ((cols, count), BF16)],
        "far_scores",
    )
    far = (keep + swap_core(give).astype(F32)).astype(BF16)
    (give,) = local_call(
        give_score_body, (loaded, corrected_cols), [(quarter, BF16)], "give_scores"
    )
    far, corrected_cols, source = lax.optimization_barrier((far, corrected_cols, features))
    (keep,) = local_call(
        keep_score_body,
        (source, corrected_cols),
        [(quarter, F32)],
        "keep_scores",
        [pltpu.VMEM((row_count // 4, cols), BF16), pltpu.SemaphoreType.DMA((4,))],
        outside=1,
        limit=46,
    )
    size = row_count // 8
    got = jnp.concatenate([swap_core(give[:size]), swap_core(give[size:])])
    return keep + got.astype(F32) + swap_chip(far).astype(F32)


def solution(mesh):
    in_specs = (P("wide", "feat"), P(), P("feat", "wide", None))
    out_specs = P(("wide", "feat"), None)
    return jax.shard_map(
        on_device, mesh=mesh, in_specs=in_specs, out_specs=out_specs, check_vma=False
    )
```
